32 devices in a mesh: draws: 2 (over y), dst: 4 (over z), org: 2 (over x), st: 2 (over core).
Axes of the slice: x: 2, y: 2, z: 4, core: 2. Of those that a mesh axis runs over, the one named last changes fastest.
Arguments:
- value_now: float32 [8, 2, 64, 4096], P(('draws', 'dst'), 'org', None, 'st'), parts along dimension 0, may hold values from -90 to 490
- utility: float32 [8, 2, 64, 4096], P(('draws', 'dst'), 'org', None, 'st'), parts along dimension 0, may hold values from -6 to 6
- move_costs: float32 [8, 2, 64, 4, 128], P('draws', 'org', None, 'dst'), parts along dimension 0, may hold values from 0 to 3
- dest_blocks: int32 [8, 3], replicated, may hold values from 0 to 7, all different within a row
- row_counts: int32 [8], replicated, may hold values from 1 to 3, as said below
- transition: int32 [4096], replicated, may hold values from 0 to 4095
Outputs:
- value_next: float32 [8, 2, 64, 4096], P(('draws', 'dst'), 'org', None, 'st'), parts along dimension 0
The draws below stay inside these ranges and needn't reach their ends.
There are 2 independent parts, one for each index of `draws`. The reference program is written for one: setup_inputs(seed, part) draws one part's arguments, and reference() takes and returns one part's arrays. A program takes and returns all parts, laid end to end along the dimension named above; an argument that names none is the same for every part. Nothing has to cross between parts.
Inputs may be any that keep to these rules, and one draw needn't show every extreme that they name: `dest_blocks`: each row names 3 different blocks; only the first row_counts[o] of row o count. `row_counts`: some anchor block has 3.
All inputs are finite; a program needn't handle non-finite values.
Results may differ from the reference program's by a relative error of at most 0.00095.
Values may be sent and summed in bfloat16 or wider, within the bound.
A program may use at most 64 MiB of HBM per device.

```python
import jax
import jax.numpy as jnp
from jax import lax

S = 4096
BLK = 64
DEST_SHARDS = 4
ORIG_SHARDS = 2
NBLK = 8
NNZ = 3
LOCATIONS = 512


def draw_value_now(key, part):
    first_key = jax.random.fold_in(key, 0)
    shape_full = (DEST_SHARDS, ORIG_SHARDS, BLK, S)
    rough = jax.random.normal(first_key, shape_full, jnp.float32)
    drawn = 2.0 * rough
    return jnp.clip(drawn, -90.0, 490.0)


def draw_row_counts(key, part):
    first_key, second_key = jax.random.split(jax.random.fold_in(key, 11))
    counts_drawn = jax.random.randint(first_key, (NBLK,), 1, NNZ + 1, dtype=jnp.int32)
    fullest = jax.random.randint(second_key, (), 0, NBLK, dtype=jnp.int32)
    return counts_drawn.at[fullest].set(NNZ)


def place_ends(result, own_key, smallest, top_value):
    index_at = [jax.random.randint(jax.random.fold_in(own_key, axis), (), 0, length) for axis, length in enumerate(result.shape)]
    widest = result.shape.index(max(result.shape))
    neighbour = index_at[:widest] + [(index_at[widest] + 1) % result.shape[widest]] + index_at[widest + 1:]
    return result.at[tuple(index_at)].set(smallest).at[tuple(neighbour)].set(top_value)


def shard_levels(stream_key, extent, shards, least, largest):
    def one(axis_at, shards_of):
        steps = jax.random.uniform(jax.random.fold_in(jax.random.fold_in(stream_key, 6), axis_at), (shards_of,), jnp.float32, least / len(shards), largest / len(shards))
        return jnp.repeat(jnp.exp(steps), extent[axis_at] // shards_of).reshape((-1,) + (1,) * (len(extent) - axis_at - 1))

    factor_of = one(*shards[0])
    for cut in shards[1:]:
        factor_of = factor_of * one(*cut)
    return factor_of


def different_ones(own_key, rows, count, top, lift):
    ranking = jax.random.permutation(jax.random.fold_in(own_key, 1), count)
    pull = ranking
    for power in range(3):
        pull = pull * pull // count
    pull = pull * lift // count
    lots = jax.random.randint(jax.random.fold_in(own_key, 2), (rows, count), 0, 4096) + pull
    sure = jax.random.permutation(jax.random.fold_in(own_key, 3), rows)[jnp.arange(count) % rows]
    lots = jnp.where(jnp.arange(rows)[:, None] == sure[None, :], 1 << 14, lots)
    score = lots * count + jnp.arange(count)
    return lax.top_k(score.astype(jnp.int32), top)[1].astype(jnp.int32)


def scatter_about(own_key, shape, scale, limit, cuts=(), held_as=jnp.bfloat16):
    loudness = shard_levels(own_key, shape, cuts, -0.22, 0.18) if cuts else 1.0
    values = jax.random.normal(own_key, shape, jnp.float32) * scale * loudness
    return jnp.minimum(jnp.maximum(values, -limit), limit).astype(held_as)


def setup_inputs(seed: int = 0, part: int = 0) -> dict:
    arg_keys = jax.random.split(jax.random.key(seed), 7)
    own_keys = jax.random.split(jax.random.fold_in(arg_keys[6], part), 7)
    value_now = draw_value_now(jax.random.fold_in(jax.random.fold_in(arg_keys[6], part), 71), part)
    utility = scatter_about(own_keys[1], (DEST_SHARDS, ORIG_SHARDS, BLK, S), 1.0, 6.0, ((0, 4), (1, 2), (3, 2)), jnp.float32)
    move_costs = jnp.clip(3.0 * jax.random.uniform(own_keys[2], (DEST_SHARDS, ORIG_SHARDS, BLK, DEST_SHARDS, ORIG_SHARDS * BLK), jnp.float32) ** shard_levels(own_keys[2], (DEST_SHARDS, ORIG_SHARDS, BLK, DEST_SHARDS, ORIG_SHARDS * BLK), ((1, 2), (3, 4)), -0.2, 0.2), 0.0, 3.0)
    dest_blocks = different_ones(arg_keys[3], NBLK, NBLK, NNZ, 6144)
    row_counts = draw_row_counts(jax.random.fold_in(arg_keys[6], 71), part)
    transition = place_ends(jax.random.randint(arg_keys[5], (S,), 0, S), jax.random.fold_in(arg_keys[5], 1), 0, S - 1).astype(jnp.int32)
    return {"value_now": value_now, "utility": utility, "move_costs": move_costs, "dest_blocks": dest_blocks, "row_counts": row_counts, "transition": transition}


DISCOUNT = 0.95
FLOOR = -1.0e30


def reference(value_now, utility, move_costs, dest_blocks, row_counts, transition):
    shifted = jnp.take(value_now.reshape(LOCATIONS, S), transition, axis=1)
    by_block = shifted.reshape(NBLK, BLK, S)
    cost_blocks = move_costs.reshape(NBLK, BLK, NBLK, BLK)
    slot_ids = jnp.arange(NNZ, dtype=jnp.int32)
    group_ids = jnp.arange(DEST_SHARDS, dtype=jnp.int32)

    def anchor_block(anchor):
        listed = dest_blocks[anchor]
        usable = slot_ids < row_counts[anchor]
        dest_rows = by_block[listed]
        block_top = jnp.max(dest_rows, axis=1)
        ceiling = jnp.max(jnp.where(usable[:, None], block_top, FLOOR), axis=0)
        weights = jnp.where(usable[:, None, None], jnp.exp(dest_rows - ceiling[None, None, :]), 0.0).astype(jnp.bfloat16)
        kernel = jnp.exp(-cost_blocks[anchor][:, listed, :]).astype(jnp.bfloat16)
        products = jnp.einsum("inj,njs->nis", kernel.astype(jnp.float32), weights.astype(jnp.float32))
        group_of = listed // ORIG_SHARDS
        group_table = (group_of[:, None] == group_ids[None, :]).astype(jnp.float32)
        partial_value = jnp.einsum("nis,nk->kis", products, group_table, precision=lax.Precision.HIGHEST).astype(jnp.bfloat16)
        merged = jnp.sum(partial_value.astype(jnp.float32), axis=0)
        return ceiling, merged

    ceilings, merged_all = lax.map(anchor_block, jnp.arange(NBLK, dtype=jnp.int32))
    value_next = utility.reshape(NBLK, BLK, S) + DISCOUNT * (ceilings[:, None, :] + jnp.log(merged_all))
    return value_next.reshape(DEST_SHARDS, ORIG_SHARDS, BLK, S)
```

```python
import functools

import jax
import jax.numpy as jnp
from jax import lax
from jax.experimental import pallas as pl
from jax.experimental.pallas import tpu as pltpu
from jax.sharding import PartitionSpec as P

DISCOUNT = 0.95
FLOOR = -1e30
TILE = 256
CHUNK = 512
AHEAD = 2
MESH = pl.DeviceIdType.MESH


def sweep(
    sizes, v_ref, cost_ref, trans_ref, lists_ref, counts_ref, out_ref,
    raw, raw_top, kern_out, kern_in, onehot, wbuf, tops, own_sum, own_top,
    x_out, x_out_top, x_in, x_in_top, reach,
    st_send, st_recv, k_send, k_recv, t_send, t_recv, up_send, dn_send, w_recv, x_send, x_recv,
):
    n_dst, n_org, n_st = sizes
    rows, states = v_ref.shape
    tiles = states // TILE
    chunks, width = wbuf.shape[1], wbuf.shape[3]
    slots = lists_ref.shape[1]
    p = lax.axis_index("dst")
    q = lax.axis_index("org")
    h = lax.axis_index("st")

    def remote(source, target, send, recv, **where):
        return pltpu.make_async_remote_copy(
            src_ref=source, dst_ref=target, send_sem=send, recv_sem=recv,
            device_id=where, device_id_type=MESH,
        )

    peers = [(a, b) for a in range(n_dst) for b in range(n_org) if (a, b) != (0, 0)]
    barrier = pltpu.get_barrier_semaphore()
    for dp, dq in peers:
        pl.semaphore_signal(
            barrier, inc=1, device_id_type=MESH,
            device_id={"dst": lax.rem(p + dp, n_dst), "org": lax.rem(q + dq, n_org)},
        )
    for d in range(1, n_st):
        pl.semaphore_signal(
            barrier, inc=1, device_id_type=MESH, device_id={"st": lax.rem(h + d, n_st)}
        )

    for t in range(tiles):
        x = v_ref[:, t * TILE:(t + 1) * TILE]
        top = jnp.max(x, axis=0, keepdims=True).astype(jnp.bfloat16).astype(jnp.float32)
        raw[h, t] = jnp.exp(x - top).astype(jnp.bfloat16)
        raw_top[h, t:t + 1, :] = top

    pl.semaphore_wait(barrier, len(peers) + n_st - 1)

    st_copies = []
    for d in range(1, n_st):
        other = lax.rem(h + d, n_st)
        for i, buf in enumerate((raw_top, raw)):
            st_copies.append(remote(
                buf.at[h], buf.at[h], st_send.at[d - 1, i], st_recv.at[d - 1, i], st=other))
            st_copies[-1].start()

    for a in range(n_dst):
        k = jnp.exp(-cost_ref[a]).astype(jnp.bfloat16)
        for b in range(n_org):
            kern_out[a, b] = k[:, b * rows:(b + 1) * rows]
    k_copies = []
    for i, (dp, dq) in enumerate(peers):
        to_p, to_q = lax.rem(p + dp, n_dst), lax.rem(q + dq, n_org)
        k_copies.append(remote(
            kern_out.at[to_p, to_q], kern_in.at[p, (n_org - dq) % n_org],
            k_send.at[i], k_recv.at[i], dst=to_p, org=to_q))
        k_copies[-1].start()
    kern_in[p, 0] = kern_out[p, q]

    for r in range(n_org):
        anchor = p * n_org + lax.rem(q + r, n_org)
        count = counts_ref[anchor]
        for b in range(n_dst):
            block = b * n_org + q

            def listed(k, found, anchor=anchor, block=block, count=count):
                hit = jnp.where(lists_ref[anchor, k] == block, 1, 0)
                return found + hit * jnp.where(k < count, 1, 0)

            if slots <= 4:
                found = jnp.int32(0)
                for k in range(slots):
                    found = listed(k, found)
            else:
                found = lax.fori_loop(0, slots, listed, jnp.int32(0))
            reach[r, b] = found.astype(jnp.float32)

    mine = trans_ref[:, pl.ds(pl.multiple_of(h * states, TILE), states)]
    low = jnp.bitwise_and(mine, TILE - 1)
    high = jnp.right_shift(mine, TILE.bit_length() - 1)
    for c in range(chunks):
        part = slice(c * width, (c + 1) * width)
        row_ids = lax.broadcasted_iota(jnp.int32, (TILE, width), 0)
        onehot[c] = jnp.where(row_ids == low[:, part], 1.0, 0.0).astype(jnp.bfloat16)

    for copy in st_copies:
        copy.wait_recv()

    total_tiles = n_st * tiles
    for c in range(chunks):
        part = slice(c * width, (c + 1) * width)
        table = raw_top[...].reshape(total_tiles, TILE).astype(jnp.bfloat16)
        picked = jnp.dot(table, onehot[c], preferred_element_type=jnp.float32)
        tile_ids = lax.broadcasted_iota(jnp.int32, (total_tiles, width), 0)
        tops[p, c] = jnp.sum(
            jnp.where(tile_ids == high[:, part], picked, 0.0), axis=0, keepdims=True)
    t_copies = []
    for d in range(1, n_dst):
        t_copies.append(remote(
            tops.at[p], tops.at[p], t_send.at[d - 1], t_recv.at[d - 1],
            dst=lax.rem(p + d, n_dst)))
        t_copies[-1].start()

    def gather(c):
        part = slice(c * width, (c + 1) * width)
        table = raw[...].reshape(total_tiles * rows, TILE)
        picked = jnp.dot(table, onehot[c], preferred_element_type=jnp.float32)
        total = picked[:rows]
        for t in range(1, total_tiles):
            total = jnp.where(high[:, part] == t, picked[t * rows:(t + 1) * rows], total)
        wbuf[p, c] = total.astype(jnp.bfloat16)

    def upward(b, c):
        return remote(wbuf.at[b, c], wbuf.at[b, c], up_send.at[b, c], w_recv.at[b, c],
                      dst=lax.rem(p + 1, n_dst))

    def downward(b, c):
        return remote(wbuf.at[b, c], wbuf.at[b, c], dn_send.at[b, c], w_recv.at[b, c],
                      dst=lax.rem(p + n_dst - 1, n_dst))

    not_last, not_first = p < n_dst - 1, p > 0

    def send_own(c):
        @pl.when(not_last)
        def _():
            upward(p, c).start()

        @pl.when(not_first)
        def _():
            downward(p, c).start()

    def relay(d, c):
        @pl.when(p >= d)
        def _():
            upward(p - d, c).wait_recv()

        @pl.when((p >= d) & not_last)
        def _():
            upward(p - d, c).start()

        @pl.when(p + d < n_dst)
        def _():
            downward(p + d, c).wait_recv()

        @pl.when((p + d < n_dst) & not_first)
        def _():
            downward(p + d, c).start()

    x_copies = {}

    def products(c):
        sums = [None] * n_org
        for r in range(n_org):
            shifted = [tops[b, c] + (reach[r, b] - 1.0) * -FLOOR for b in range(n_dst)]
            ceiling = functools.reduce(jnp.maximum, shifted)
            total = None
            for b in range(n_dst):
                scale = reach[r, b] * jnp.exp(shifted[b] - ceiling)
                term = scale * jnp.dot(
                    kern_in[b, r], wbuf[b, c], preferred_element_type=jnp.float32)
                total = term if total is None else total + term
            sums[r] = total
            if r == 0:
                own_sum[c] = total
                own_top[c] = ceiling
            else:
                x_out[r - 1, c] = total.astype(jnp.bfloat16)
                x_out_top[r - 1, c] = ceiling
                to = lax.rem(q + r, n_org)
                for i, (src, dst) in enumerate(((x_out_top, x_in_top), (x_out, x_in))):
                    copy = remote(src.at[r - 1, c], dst.at[r - 1, c],
                                  x_send.at[r - 1, c, i], x_recv.at[r - 1, c, i], org=to)
                    copy.start()
                    x_copies.setdefault(c, []).append(copy)

    def finish(c):
        for copy in x_copies.get(c, []):
            copy.wait_recv()
        ceiling = own_top[c]
        for r in range(1, n_org):
            ceiling = jnp.maximum(ceiling, x_in_top[r - 1, c])
        merged = jnp.exp(own_top[c] - ceiling) * own_sum[c]
        for r in range(1, n_org):
            merged += jnp.exp(x_in_top[r - 1, c] - ceiling) * x_in[r - 1, c].astype(jnp.float32)
        out_ref[:, c * width:(c + 1) * width] = DISCOUNT * (ceiling + jnp.log(merged))

    for c in range(min(AHEAD, chunks)):
        gather(c)
        send_own(c)
    for c in range(AHEAD, chunks):
        gather(c)
    for copy in k_copies:
        copy.wait_recv()
    for copy in t_copies:
        copy.wait_recv()
    for c in range(chunks):
        for d in range(1, n_dst):
            relay(d, c)
            if d == 1 and c + AHEAD < chunks:
                send_own(c + AHEAD)
        products(c)
        if c > 0:
            finish(c - 1)
    finish(chunks - 1)

    for copy in st_copies + k_copies + t_copies:
        copy.wait_send()
    for c in range(chunks):
        for d in range(n_dst):
            @pl.when((p >= d) & not_last)
            def _(d=d, c=c):
                upward(p - d, c).wait_send()

            @pl.when((p + d < n_dst) & not_first)
            def _(d=d, c=c):
                downward(p + d, c).wait_send()

        for copy in x_copies.get(c, []):
            copy.wait_send()


def on_device(sizes, value_now, utility, move_costs, dest_blocks, row_counts, transition):
    n_dst, n_org, n_st = sizes
    rows, states = value_now.shape[2:]
    width = min(CHUNK, states)
    chunks = states // width
    tiles = states // TILE
    peers = n_dst * n_org - 1
    others = max(n_org - 1, 1)
    vmem = pl.BlockSpec(memory_space=pltpu.VMEM)
    smem = pl.BlockSpec(memory_space=pltpu.SMEM)
    dma = pltpu.SemaphoreType.DMA
    bf16, f32 = jnp.bfloat16, jnp.float32
    partial = pl.pallas_call(
        functools.partial(sweep, sizes),
        out_shape=jax.ShapeDtypeStruct((rows, states), f32),
        in_specs=[vmem, vmem, vmem, smem, smem],
        out_specs=vmem,
        scratch_shapes=[
            pltpu.VMEM((n_st, tiles, rows, TILE), bf16),
            pltpu.VMEM((n_st, tiles, TILE), f32),
            pltpu.VMEM((n_dst, n_org, rows, rows), bf16),
            pltpu.VMEM((n_dst, n_org, rows, rows), bf16),
            pltpu.VMEM((chunks, TILE, width), bf16),
            pltpu.VMEM((n_dst, chunks, rows, width), bf16),
            pltpu.VMEM((n_dst, chunks, 1, width), f32),
            pltpu.VMEM((chunks, rows, width), f32),
            pltpu.VMEM((chunks, 1, width), f32),
            pltpu.VMEM((others, chunks, rows, width), bf16),
            pltpu.VMEM((others, chunks, 1, width), f32),
            pltpu.VMEM((others, chunks, rows, width), bf16),
            pltpu.VMEM((others, chunks, 1, width), f32),
            pltpu.SMEM((n_org, n_dst), f32),
            dma((max(n_st - 1, 1), 2)), dma((max(n_st - 1, 1), 2)),
            dma((max(peers, 1),)), dma((max(peers, 1),)),
            dma((max(n_dst - 1, 1),)), dma((max(n_dst - 1, 1),)),
            dma((n_dst, chunks)), dma((n_dst, chunks)), dma((n_dst, chunks)),
            dma((others, chunks, 2)), dma((others, chunks, 2)),
        ],
        compiler_params=pltpu.CompilerParams(
            collective_id=0, has_side_effects=True, vmem_limit_bytes=48 * 2**20
        ),
    )(
        value_now.reshape(rows, states),
        move_costs.reshape(n_dst, rows, n_org * rows),
        transition.reshape(1, -1),
        dest_blocks,
        row_counts,
    )
    return utility + partial[None, None]


def solution(mesh):
    sizes = tuple(mesh.shape[axis] for axis in ("dst", "org", "st"))
    return jax.shard_map(
        functools.partial(on_device, sizes),
        mesh=mesh,
        in_specs=(
            P(("draws", "dst"), "org", None, "st"),
            P(("draws", "dst"), "org", None, "st"),
            P("draws", "org", None, "dst", None),
            P(),
            P(),
            P(),
        ),
        out_specs=P(("draws", "dst"), "org", None, "st"),
        check_vma=False,
    )
```

```python
import functools

import jax
import jax.numpy as jnp
from jax import lax
from jax.experimental import pallas as pl
from jax.experimental.pallas import tpu as pltpu
from jax.sharding import PartitionSpec as P

DISCOUNT = 0.95
FLOOR = -1e30
TILE = 256
CHUNK = 512
AHEAD = 2
MESH = pl.DeviceIdType.MESH


def sweep(
    sizes, v_in, cost_in, trans_in, lists_in, counts_in, out_ref,
    v_ref, cost_ref, trans_ref, lists_ref, counts_ref, in_sem,
    raw, raw_top, kern_out, kern_in, onehot, wbuf, tops, own_sum, own_top,
    x_out, x_out_top, x_in, x_in_top, reach,
    st_send, st_recv, k_send, k_recv, t_send, t_recv, up_send, dn_send, w_recv, x_send, x_recv,
):
    n_dst, n_org, n_st = sizes
    rows, states = v_ref.shape
    tiles = states // TILE
    chunks, width = wbuf.shape[1], wbuf.shape[3]
    slots = lists_ref.shape[0]
    p = lax.axis_index("dst")
    q = lax.axis_index("org")
    h = lax.axis_index("st")

    def remote(source, target, send, recv, **where):
        return pltpu.make_async_remote_copy(
            src_ref=source, dst_ref=target, send_sem=send, recv_sem=recv,
            device_id=where, device_id_type=MESH,
        )

    fetches = [
        pltpu.make_async_copy(source, target, in_sem.at[i])
        for i, (source, target) in enumerate((
            (v_in, v_ref), (cost_in, cost_ref), (trans_in, trans_ref),
            (lists_in, lists_ref), (counts_in, counts_ref)))
    ]
    for fetch in fetches:
        fetch.start()
    peers = [(a, b) for a in range(n_dst) for b in range(n_org) if (a, b) != (0, 0)]
    barrier = pltpu.get_barrier_semaphore()
    for dp, dq in peers:
        pl.semaphore_signal(
            barrier, inc=1, device_id_type=MESH,
            device_id={"dst": lax.rem(p + dp, n_dst), "org": lax.rem(q + dq, n_org)},
        )
    for d in range(1, n_st):
        pl.semaphore_signal(
            barrier, inc=1, device_id_type=MESH, device_id={"st": lax.rem(h + d, n_st)}
        )

    fetches[0].wait()
    for t in range(tiles):
        x = v_ref[:, t * TILE:(t + 1) * TILE]
        top = jnp.max(x, axis=0, keepdims=True).astype(jnp.bfloat16).astype(jnp.float32)
        raw[h, t] = jnp.exp(x - top).astype(jnp.bfloat16)
        raw_top[h, t:t + 1, :] = top

    pl.semaphore_wait(barrier, len(peers) + n_st - 1)

    st_copies = []
    for d in range(1, n_st):
        other = lax.rem(h + d, n_st)
        for i, buf in enumerate((raw_top, raw)):
            st_copies.append(remote(
                buf.at[h], buf.at[h], st_send.at[d - 1, i], st_recv.at[d - 1, i], st=other))
            st_copies[-1].start()

    for fetch in fetches[1:]:
        fetch.wait()
    for a in range(n_dst):
        k = jnp.exp(-cost_ref[a]).astype(jnp.bfloat16)
        for b in range(n_org):
            kern_out[a, b] = k[:, b * rows:(b + 1) * rows]
    k_copies = []
    for i, (dp, dq) in enumerate(peers):
        to_p, to_q = lax.rem(p + dp, n_dst), lax.rem(q + dq, n_org)
        k_copies.append(remote(
            kern_out.at[to_p, to_q], kern_in.at[p, (n_org - dq) % n_org],
            k_send.at[i], k_recv.at[i], dst=to_p, org=to_q))
        k_copies[-1].start()
    kern_in[p, 0] = kern_out[p, q]

    for r in range(n_org):
        anchor = p * n_org + lax.rem(q + r, n_org)
        count = counts_ref[anchor]
        for b in range(n_dst):
            block = b * n_org + q

            def listed(k, found, anchor=anchor, block=block, count=count):
                hit = jnp.where(lists_ref[k, anchor] == block, 1, 0)
                return found + hit * jnp.where(k < count, 1, 0)

            if slots <= 4:
                found = jnp.int32(0)
                for k in range(slots):
                    found = listed(k, found)
            else:
                found = lax.fori_loop(0, slots, listed, jnp.int32(0))
            reach[r, b] = found.astype(jnp.float32)

    mine = trans_ref[:, pl.ds(pl.multiple_of(h * states, TILE), states)]
    low = jnp.bitwise_and(mine, TILE - 1)
    high = jnp.right_shift(mine, TILE.bit_length() - 1)
    for c in range(chunks):
        part = slice(c * width, (c + 1) * width)
        row_ids = lax.broadcasted_iota(jnp.int32, (TILE, width), 0)
        onehot[c] = jnp.where(row_ids == low[:, part], 1.0, 0.0).astype(jnp.bfloat16)

    for copy in st_copies:
        copy.wait_recv()

    total_tiles = n_st * tiles
    for c in range(chunks):
        part = slice(c * width, (c + 1) * width)
        table = raw_top[...].reshape(total_tiles, TILE).astype(jnp.bfloat16)
        picked = jnp.dot(table, onehot[c], preferred_element_type=jnp.float32)
        tile_ids = lax.broadcasted_iota(jnp.int32, (total_tiles, width), 0)
        tops[p, c] = jnp.sum(
            jnp.where(tile_ids == high[:, part], picked, 0.0), axis=0, keepdims=True)
    t_copies = []
    for d in range(1, n_dst):
        t_copies.append(remote(
            tops.at[p], tops.at[p], t_send.at[d - 1], t_recv.at[d - 1],
            dst=lax.rem(p + d, n_dst)))
        t_copies[-1].start()

    def gather(c):
        part = slice(c * width, (c + 1) * width)
        table = raw[...].reshape(total_tiles * rows, TILE)
        picked = jnp.dot(table, onehot[c], preferred_element_type=jnp.float32)
        total = picked[:rows]
        for t in range(1, total_tiles):
            total = jnp.where(high[:, part] == t, picked[t * rows:(t + 1) * rows], total)
        wbuf[p, c] = total.astype(jnp.bfloat16)

    def upward(b, c):
        return remote(wbuf.at[b, c], wbuf.at[b, c], up_send.at[b, c], w_recv.at[b, c],
                      dst=lax.rem(p + 1, n_dst))

    def downward(b, c):
        return remote(wbuf.at[b, c], wbuf.at[b, c], dn_send.at[b, c], w_recv.at[b, c],
                      dst=lax.rem(p + n_dst - 1, n_dst))

    not_last, not_first = p < n_dst - 1, p > 0

    def send_own(c):
        @pl.when(not_last)
        def _():
            upward(p, c).start()

        @pl.when(not_first)
        def _():
            downward(p, c).start()

    def relay(d, c):
        @pl.when(p >= d)
        def _():
            upward(p - d, c).wait_recv()

        @pl.when((p >= d) & not_last)
        def _():
            upward(p - d, c).start()

        @pl.when(p + d < n_dst)
        def _():
            downward(p + d, c).wait_recv()

        @pl.when((p + d < n_dst) & not_first)
        def _():
            downward(p + d, c).start()

    x_copies = {}

    def products(c):
        sums = [None] * n_org
        for r in range(n_org):
            shifted = [tops[b, c] + (reach[r, b] - 1.0) * -FLOOR for b in range(n_dst)]
            ceiling = functools.reduce(jnp.maximum, shifted)
            total = None
            for b in range(n_dst):
                scale = reach[r, b] * jnp.exp(shifted[b] - ceiling)
                term = scale * jnp.dot(
                    kern_in[b, r], wbuf[b, c], preferred_element_type=jnp.float32)
                total = term if total is None else total + term
            sums[r] = total
            if r == 0:
                own_sum[c] = total
                own_top[c] = ceiling
            else:
                x_out[r - 1, c] = total.astype(jnp.bfloat16)
                x_out_top[r - 1, c] = ceiling
                to = lax.rem(q + r, n_org)
                for i, (src, dst) in enumerate(((x_out_top, x_in_top), (x_out, x_in))):
                    copy = remote(src.at[r - 1, c], dst.at[r - 1, c],
                                  x_send.at[r - 1, c, i], x_recv.at[r - 1, c, i], org=to)
                    copy.start()
                    x_copies.setdefault(c, []).append(copy)

    def finish(c):
        for copy in x_copies.get(c, []):
            copy.wait_recv()
        ceiling = own_top[c]
        for r in range(1, n_org):
            ceiling = jnp.maximum(ceiling, x_in_top[r - 1, c])
        merged = jnp.exp(own_top[c] - ceiling) * own_sum[c]
        for r in range(1, n_org):
            merged += jnp.exp(x_in_top[r - 1, c] - ceiling) * x_in[r - 1, c].astype(jnp.float32)
        out_ref[:, c * width:(c + 1) * width] = DISCOUNT * (ceiling + jnp.log(merged))

    for c in range(min(AHEAD, chunks)):
        gather(c)
        send_own(c)
    for c in range(AHEAD, chunks):
        gather(c)
    for copy in k_copies:
        copy.wait_recv()
    for copy in t_copies:
        copy.wait_recv()
    for wave in range(chunks + n_dst - 2):
        for d in range(1, n_dst):
            c = wave - d + 1
            if 0 <= c < chunks:
                relay(d, c)
                if d == 1 and c + AHEAD < chunks:
                    send_own(c + AHEAD)
        done = wave - n_dst + 2
        if done >= 0:
            products(done)
        if done >= 1:
            finish(done - 1)
    finish(chunks - 1)

    for copy in st_copies + k_copies + t_copies:
        copy.wait_send()
    for c in range(chunks):
        for d in range(n_dst):
            @pl.when((p >= d) & not_last)
            def _(d=d, c=c):
                upward(p - d, c).wait_send()

            @pl.when((p + d < n_dst) & not_first)
            def _(d=d, c=c):
                downward(p + d, c).wait_send()

        for copy in x_copies.get(c, []):
            copy.wait_send()


def on_device(sizes, value_now, utility, move_costs, dest_blocks, row_counts, transition):
    n_dst, n_org, n_st = sizes
    rows, states = value_now.shape[2:]
    width = min(CHUNK, states)
    chunks = states // width
    tiles = states // TILE
    peers = n_dst * n_org - 1
    others = max(n_org - 1, 1)
    vmem = pl.BlockSpec(memory_space=pltpu.VMEM)
    hbm = pl.BlockSpec(memory_space=pltpu.HBM)
    dma = pltpu.SemaphoreType.DMA
    bf16, f32 = jnp.bfloat16, jnp.float32
    partial = pl.pallas_call(
        functools.partial(sweep, sizes),
        out_shape=jax.ShapeDtypeStruct((rows, states), f32),
        in_specs=[hbm] * 5,
        out_specs=vmem,
        scratch_shapes=[
            pltpu.VMEM((rows, states), f32),
            pltpu.VMEM((n_dst, rows, n_org * rows), f32),
            pltpu.VMEM((1, transition.shape[0]), jnp.int32),
            pltpu.SMEM(dest_blocks.shape[::-1], jnp.int32),
            pltpu.SMEM(row_counts.shape, jnp.int32),
            dma((5,)),
            pltpu.VMEM((n_st, tiles, rows, TILE), bf16),
            pltpu.VMEM((n_st, tiles, TILE), f32),
            pltpu.VMEM((n_dst, n_org, rows, rows), bf16),
            pltpu.VMEM((n_dst, n_org, rows, rows), bf16),
            pltpu.VMEM((chunks, TILE, width), bf16),
            pltpu.VMEM((n_dst, chunks, rows, width), bf16),
            pltpu.VMEM((n_dst, chunks, 1, width), f32),
            pltpu.VMEM((chunks, rows, width), f32),
            pltpu.VMEM((chunks, 1, width), f32),
            pltpu.VMEM((others, chunks, rows, width), bf16),
            pltpu.VMEM((others, chunks, 1, width), f32),
            pltpu.VMEM((others, chunks, rows, width), bf16),
            pltpu.VMEM((others, chunks, 1, width), f32),
            pltpu.SMEM((n_org, n_dst), f32),
            dma((max(n_st - 1, 1), 2)), dma((max(n_st - 1, 1), 2)),
            dma((max(peers, 1),)), dma((max(peers, 1),)),
            dma((max(n_dst - 1, 1),)), dma((max(n_dst - 1, 1),)),
            dma((n_dst, chunks)), dma((n_dst, chunks)), dma((n_dst, chunks)),
            dma((others, chunks, 2)), dma((others, chunks, 2)),
        ],
        compiler_params=pltpu.CompilerParams(
            collective_id=0, has_side_effects=True, vmem_limit_bytes=63 * 2**20
        ),
    )(
        value_now.reshape(rows, states),
        move_costs.reshape(n_dst, rows, n_org * rows),
        transition.reshape(1, -1),
        dest_blocks.T,
        row_counts,
    )
    return utility + partial[None, None]


def solution(mesh):
    sizes = tuple(mesh.shape[axis] for axis in ("dst", "org", "st"))
    return jax.shard_map(
        functools.partial(on_device, sizes),
        mesh=mesh,
        in_specs=(
            P(("draws", "dst"), "org", None, "st"),
            P(("draws", "dst"), "org", None, "st"),
            P("draws", "org", None, "dst", None),
            P(),
            P(),
            P(),
        ),
        out_specs=P(("draws", "dst"), "org", None, "st"),
        check_vma=False,
    )
```

```python
import functools

import jax
import jax.numpy as jnp
from jax import lax
from jax.experimental import pallas as pl
from jax.experimental.pallas import tpu as pltpu
from jax.sharding import PartitionSpec as P

DISCOUNT = 0.95
FLOOR = -1e30
TILE = 256
CHUNK = 256
AHEAD = 3
MESH = pl.DeviceIdType.MESH


def sweep(
    sizes, v_in, cost_in, trans_in, lists_in, counts_in, out_ref,
    v_ref, cost_ref, trans_ref, lists_ref, counts_ref, in_sem,
    raw, raw_top, kern_out, kern_in, onehot, wbuf, tops, own_sum, own_top,
    x_out, x_out_top, x_in, x_in_top, z_out, z_out_top, z_in, z_in_top, reach,
    st_send, st_recv, k_send, k_recv, t_send, t_recv, up_send, dn_send, w_recv, x_send, x_recv,
    z_send, z_recv,
):
    n_dst, n_org, n_st = sizes
    rows, states = v_ref.shape
    tiles = states // TILE
    chunks, width = wbuf.shape[1], wbuf.shape[3]
    slots = lists_ref.shape[0]
    p = lax.axis_index("dst")
    q = lax.axis_index("org")
    h = lax.axis_index("st")
    last = n_dst - 1
    inner = (p > 0) & (p < last)
    server = (p == 1) | (p == last - 1)
    served = jnp.where(p == 1, 0, last)
    active = (inner, server)

    def remote(source, target, send, recv, **where):
        return pltpu.make_async_remote_copy(
            src_ref=source, dst_ref=target, send_sem=send, recv_sem=recv,
            device_id=where, device_id_type=MESH,
        )

    fetches = [
        pltpu.make_async_copy(source, target, in_sem.at[i])
        for i, (source, target) in enumerate((
            (v_in, v_ref), (cost_in, cost_ref), (trans_in, trans_ref),
            (lists_in, lists_ref), (counts_in, counts_ref)))
    ]
    for fetch in fetches:
        fetch.start()
    peers = [(a, b) for a in range(n_dst) for b in range(n_org) if (a, b) != (0, 0)]
    barrier = pltpu.get_barrier_semaphore()
    for dp, dq in peers:
        pl.semaphore_signal(
            barrier, inc=1, device_id_type=MESH,
            device_id={"dst": lax.rem(p + dp, n_dst), "org": lax.rem(q + dq, n_org)},
        )
    for d in range(1, n_st):
        pl.semaphore_signal(
            barrier, inc=1, device_id_type=MESH, device_id={"st": lax.rem(h + d, n_st)}
        )

    fetches[0].wait()
    for t in range(tiles):
        x = v_ref[:, t * TILE:(t + 1) * TILE]
        top = jnp.max(x, axis=0, keepdims=True).astype(jnp.bfloat16).astype(jnp.float32)
        raw[h, t] = jnp.exp(x - top).astype(jnp.bfloat16)
        raw_top[h, t:t + 1, :] = top

    pl.semaphore_wait(barrier, len(peers) + n_st - 1)

    st_copies = []
    for d in range(1, n_st):
        other = lax.rem(h + d, n_st)
        for i, buf in enumerate((raw_top, raw)):
            st_copies.append(remote(
                buf.at[h], buf.at[h], st_send.at[d - 1, i], st_recv.at[d - 1, i], st=other))
            st_copies[-1].start()

    for fetch in fetches[1:]:
        fetch.wait()
    for a in range(n_dst):
        k = jnp.exp(-cost_ref[a]).astype(jnp.bfloat16)
        for b in range(n_org):
            kern_out[a, b] = k[:, b * rows:(b + 1) * rows]

    def cost_copy(a, dq):
        target = min(max(a, 1), last - 1)
        return remote(
            kern_out.at[a, lax.rem(q + dq, n_org)],
            kern_in.at[int(a != target), p, (n_org - dq) % n_org],
            k_send.at[a, dq], k_recv.at[int(a != target), p, (n_org - dq) % n_org],
            dst=target, org=lax.rem(q + dq, n_org))

    for a in range(n_dst):
        target = min(max(a, 1), last - 1)
        for dq in range(1, n_org):
            cost_copy(a, dq).start()

        @pl.when(p != target)
        def _(a=a):
            cost_copy(a, 0).start()

        @pl.when(p == target)
        def _(a=a, target=target):
            kern_in[int(a != target), p, 0] = kern_out[a, q]

    def cost_arrivals():
        for slot in range(2):
            for b in range(n_dst):
                for r in range(n_org):
                    @pl.when(active[slot] if r else active[slot] & (p != b))
                    def _(slot=slot, b=b, r=r):
                        place = kern_in.at[slot, b, r]
                        remote(place, place, k_send.at[0, 0], k_recv.at[slot, b, r],
                               dst=lax.rem(p + 1, n_dst)).wait_recv()

    for slot, r in ((i, j) for i in range(2) for j in range(n_org)):
        anchor = (served if slot else p) * n_org + lax.rem(q + r, n_org)
        count = counts_ref[anchor]
        for b in range(n_dst):
            block = b * n_org + q

            def listed(k, found, anchor=anchor, block=block, count=count):
                hit = jnp.where(lists_ref[k, anchor] == block, 1, 0)
                return found + hit * jnp.where(k < count, 1, 0)

            if slots <= 4:
                found = jnp.int32(0)
                for k in range(slots):
                    found = listed(k, found)
            else:
                found = lax.fori_loop(0, slots, listed, jnp.int32(0))
            reach[slot, r, b] = found.astype(jnp.float32)

    mine = trans_ref[:, pl.ds(pl.multiple_of(h * states, TILE), states)]
    low = jnp.bitwise_and(mine, TILE - 1)
    high = jnp.right_shift(mine, TILE.bit_length() - 1)
    for c in range(chunks):
        part = slice(c * width, (c + 1) * width)
        row_ids = lax.broadcasted_iota(jnp.int32, (TILE, width), 0)
        onehot[c] = jnp.where(row_ids == low[:, part], 1.0, 0.0).astype(jnp.bfloat16)

    for copy in st_copies:
        copy.wait_recv()

    total_tiles = n_st * tiles
    for c in range(chunks):
        part = slice(c * width, (c + 1) * width)
        table = raw_top[...].reshape(total_tiles, TILE).astype(jnp.bfloat16)
        picked = jnp.dot(table, onehot[c], preferred_element_type=jnp.float32)
        tile_ids = lax.broadcasted_iota(jnp.int32, (total_tiles, width), 0)
        tops[p, c] = jnp.sum(
            jnp.where(tile_ids == high[:, part], picked, 0.0), axis=0, keepdims=True)
    t_copies = []
    for d in range(1, n_dst):
        t_copies.append(remote(
            tops.at[p], tops.at[p], t_send.at[d - 1], t_recv.at[d - 1],
            dst=lax.rem(p + d, n_dst)))
        t_copies[-1].start()

    def gather(c):
        part = slice(c * width, (c + 1) * width)
        table = raw[...].reshape(total_tiles * rows, TILE)
        picked = jnp.dot(table, onehot[c], preferred_element_type=jnp.float32)
        total = picked[:rows]
        for t in range(1, total_tiles):
            total = jnp.where(high[:, part] == t, picked[t * rows:(t + 1) * rows], total)
        wbuf[p, c] = total.astype(jnp.bfloat16)

    def upward(b, c):
        return remote(wbuf.at[b, c], wbuf.at[b, c], up_send.at[b, c], w_recv.at[b, c],
                      dst=lax.rem(p + 1, n_dst))

    def downward(b, c):
        return remote(wbuf.at[b, c], wbuf.at[b, c], dn_send.at[b, c], w_recv.at[b, c],
                      dst=lax.rem(p + n_dst - 1, n_dst))

    can_up, can_down = p < last - 1, p > 1

    def send_own(c):
        @pl.when(can_up)
        def _():
            upward(p, c).start()

        @pl.when(can_down)
        def _():
            downward(p, c).start()

    def relay(d, c):
        @pl.when((p >= d) & inner)
        def _():
            upward(p - d, c).wait_recv()

        @pl.when((p >= d) & can_up)
        def _():
            upward(p - d, c).start()

        @pl.when((p + d < n_dst) & inner)
        def _():
            downward(p + d, c).wait_recv()

        @pl.when((p + d < n_dst) & can_down)
        def _():
            downward(p + d, c).start()

    def across(slot, r, c):
        at = (slot, r - 1, c)
        return [
            remote(source.at[at], target.at[at], x_send.at[slot, r - 1, c, i],
                   x_recv.at[slot, r - 1, c, i], org=lax.rem(q + r, n_org))
            for i, (source, target) in enumerate(((x_out_top, x_in_top), (x_out, x_in)))
        ]

    def outward(c):
        return [
            remote(source.at[c], target.at[c], z_send.at[c, i], z_recv.at[c, i], dst=served)
            for i, (source, target) in enumerate(((z_out_top, z_in_top), (z_out, z_in)))
        ]

    def products(slot, c):
        for r in reversed(range(n_org)):
            shifted = [tops[b, c] + (reach[slot, r, b] - 1.0) * -FLOOR for b in range(n_dst)]
            ceiling = functools.reduce(jnp.maximum, shifted)
            total = None
            for b in range(n_dst):
                scale = reach[slot, r, b] * jnp.exp(shifted[b] - ceiling)
                term = scale * jnp.dot(
                    kern_in[slot, b, r], wbuf[b, c], preferred_element_type=jnp.float32)
                total = term if total is None else total + term
            if r == 0:
                own_sum[slot, c] = total
                own_top[slot, c] = ceiling
            else:
                x_out[slot, r - 1, c] = total.astype(jnp.bfloat16)
                x_out_top[slot, r - 1, c] = ceiling
                for copy in across(slot, r, c):
                    copy.start()

    def finish(slot, c):
        for r in range(1, n_org):
            for copy in across(slot, r, c):
                copy.wait_recv()
        ceiling = own_top[slot, c]
        for r in range(1, n_org):
            ceiling = jnp.maximum(ceiling, x_in_top[slot, r - 1, c])
        merged = jnp.exp(own_top[slot, c] - ceiling) * own_sum[slot, c]
        for r in range(1, n_org):
            merged += (jnp.exp(x_in_top[slot, r - 1, c] - ceiling)
                       * x_in[slot, r - 1, c].astype(jnp.float32))
        if slot:
            z_out[c] = merged.astype(jnp.bfloat16)
            z_out_top[c] = ceiling
            for copy in outward(c):
                copy.start()
        else:
            out_ref[:, c * width:(c + 1) * width] = DISCOUNT * (ceiling + jnp.log(merged))

    def both(step, c):
        for slot in (1, 0):
            @pl.when(active[slot])
            def _(slot=slot):
                step(slot, c)

    for c in range(min(AHEAD, chunks)):
        gather(c)
        send_own(c)
    for c in range(AHEAD, chunks):
        gather(c)
    cost_arrivals()
    for copy in t_copies:
        copy.wait_recv()
    for wave in range(chunks + n_dst - 3):
        for d in range(1, n_dst - 1):
            c = wave - d + 1
            if 0 <= c < chunks:
                relay(d, c)
                if d == 1 and c + AHEAD < chunks:
                    send_own(c + AHEAD)
        done = wave - n_dst + 3
        if done >= 0:
            both(products, done)
        if done >= 1:
            both(finish, done - 1)
    both(finish, chunks - 1)

    @pl.when(jnp.logical_not(inner))
    def _():
        for c in range(chunks):
            for copy in outward(c):
                copy.wait_recv()
            out_ref[:, c * width:(c + 1) * width] = DISCOUNT * (
                z_in_top[c] + jnp.log(z_in[c].astype(jnp.float32)))

    for copy in st_copies + t_copies:
        copy.wait_send()
    for a in range(n_dst):
        for dq in range(1, n_org):
            cost_copy(a, dq).wait_send()

        @pl.when(p != min(max(a, 1), last - 1))
        def _(a=a):
            cost_copy(a, 0).wait_send()

    for c in range(chunks):
        for d in range(n_dst):
            @pl.when((p >= d) & can_up)
            def _(d=d, c=c):
                upward(p - d, c).wait_send()

            @pl.when((p + d < n_dst) & can_down)
            def _(d=d, c=c):
                downward(p + d, c).wait_send()

        for slot in range(2):
            @pl.when(active[slot])
            def _(slot=slot, c=c):
                copies = [copy for r in range(1, n_org) for copy in across(slot, r, c)]
                for copy in copies + (outward(c) if slot else []):
                    copy.wait_send()


def on_device(sizes, value_now, utility, move_costs, dest_blocks, row_counts, transition):
    n_dst, n_org, n_st = sizes
    rows, states = value_now.shape[2:]
    width = min(CHUNK, states)
    chunks = states // width
    tiles = states // TILE
    others = max(n_org - 1, 1)
    vmem = pl.BlockSpec(memory_space=pltpu.VMEM)
    hbm = pl.BlockSpec(memory_space=pltpu.HBM)
    dma = pltpu.SemaphoreType.DMA
    bf16, f32 = jnp.bfloat16, jnp.float32
    partial = pl.pallas_call(
        functools.partial(sweep, sizes),
        out_shape=jax.ShapeDtypeStruct((rows, states), f32),
        in_specs=[hbm] * 5,
        out_specs=vmem,
        scratch_shapes=[
            pltpu.VMEM((rows, states), f32),
            pltpu.VMEM((n_dst, rows, n_org * rows), f32),
            pltpu.VMEM((1, transition.shape[0]), jnp.int32),
            pltpu.SMEM(dest_blocks.shape[::-1], jnp.int32),
            pltpu.SMEM(row_counts.shape, jnp.int32),
            dma((5,)),
            pltpu.VMEM((n_st, tiles, rows, TILE), bf16),
            pltpu.VMEM((n_st, tiles, TILE), f32),
            pltpu.VMEM((n_dst, n_org, rows, rows), bf16),
            pltpu.VMEM((2, n_dst, n_org, rows, rows), bf16),
            pltpu.VMEM((chunks, TILE, width), bf16),
            pltpu.VMEM((n_dst, chunks, rows, width), bf16),
            pltpu.VMEM((n_dst, chunks, 1, width), f32),
            pltpu.VMEM((2, chunks, rows, width), f32),
            pltpu.VMEM((2, chunks, 1, width), f32),
            pltpu.VMEM((2, others, chunks, rows, width), bf16),
            pltpu.VMEM((2, others, chunks, 1, width), f32),
            pltpu.VMEM((2, others, chunks, rows, width), bf16),
            pltpu.VMEM((2, others, chunks, 1, width), f32),
            pltpu.VMEM((chunks, rows, width), bf16),
            pltpu.VMEM((chunks, 1, width), f32),
            pltpu.VMEM((chunks, rows, width), bf16),
            pltpu.VMEM((chunks, 1, width), f32),
            pltpu.SMEM((2, n_org, n_dst), f32),
            dma((max(n_st - 1, 1), 2)), dma((max(n_st - 1, 1), 2)),
            dma((n_dst, n_org)), dma((2, n_dst, n_org)),
            dma((max(n_dst - 1, 1),)), dma((max(n_dst - 1, 1),)),
            dma((n_dst, chunks)), dma((n_dst, chunks)), dma((n_dst, chunks)),
            dma((2, others, chunks, 2)), dma((2, others, chunks, 2)),
            dma((chunks, 2)), dma((chunks, 2)),
        ],
        compiler_params=pltpu.CompilerParams(
            collective_id=0, has_side_effects=True, vmem_limit_bytes=63 * 2**20
        ),
    )(
        value_now.reshape(rows, states),
        move_costs.reshape(n_dst, rows, n_org * rows),
        transition.reshape(1, -1),
        dest_blocks.T,
        row_counts,
    )
    return utility + partial[None, None]


def solution(mesh):
    sizes = tuple(mesh.shape[axis] for axis in ("dst", "org", "st"))
    return jax.shard_map(
        functools.partial(on_device, sizes),
        mesh=mesh,
        in_specs=(
            P(("draws", "dst"), "org", None, "st"),
            P(("draws", "dst"), "org", None, "st"),
            P("draws", "org", None, "dst", None),
            P(),
            P(),
            P(),
        ),
        out_specs=P(("draws", "dst"), "org", None, "st"),
        check_vma=False,
    )
```

```python
import functools

import jax
import jax.numpy as jnp
from jax import lax
from jax.experimental import pallas as pl
from jax.experimental.pallas import tpu as pltpu
from jax.sharding import PartitionSpec as P

DISCOUNT = 0.95
FLOOR = -1e30
TILE = 256
CHUNK = 512
AHEAD = 2
MESH = pl.DeviceIdType.MESH


def sweep(
    sizes, v_in, cost_in, trans_in, lists_in, counts_in, out_ref,
    v_ref, cost_ref, trans_ref, lists_ref, counts_ref, in_sem,
    raw, raw_top, kern_out, kern_in, onehot, wbuf, tops, own_sum, own_top,
    x_out, x_out_top, x_in, x_in_top, z_out, z_out_top, z_in, z_in_top, reach,
    st_send, st_recv, k_send, k_recv, t_send, t_recv, up_send, dn_send, w_recv, x_send, x_recv,
    z_send, z_recv,
):
    n_dst, n_org, n_st = sizes
    rows, states = v_ref.shape
    tiles = states // TILE
    chunks, width = wbuf.shape[1], wbuf.shape[3]
    slots = lists_ref.shape[0]
    p = lax.axis_index("dst")
    q = lax.axis_index("org")
    h = lax.axis_index("st")
    last = n_dst - 1
    inner = (p > 0) & (p < last)
    server = (p == 1) | (p == last - 1)
    served = jnp.where(p == 1, 0, last)
    active = (inner, server)

    def remote(source, target, send, recv, **where):
        return pltpu.make_async_remote_copy(
            src_ref=source, dst_ref=target, send_sem=send, recv_sem=recv,
            device_id=where, device_id_type=MESH,
        )

    fetches = [
        pltpu.make_async_copy(source, target, in_sem.at[i])
        for i, (source, target) in enumerate((
            (v_in, v_ref), (cost_in, cost_ref), (trans_in, trans_ref),
            (lists_in, lists_ref), (counts_in, counts_ref)))
    ]
    for fetch in fetches:
        fetch.start()
    peers = [(a, b) for a in range(n_dst) for b in range(n_org) if (a, b) != (0, 0)]
    barrier = pltpu.get_barrier_semaphore()
    for dp, dq in peers:
        pl.semaphore_signal(
            barrier, inc=1, device_id_type=MESH,
            device_id={"dst": lax.rem(p + dp, n_dst), "org": lax.rem(q + dq, n_org)},
        )
    for d in range(1, n_st):
        pl.semaphore_signal(
            barrier, inc=1, device_id_type=MESH, device_id={"st": lax.rem(h + d, n_st)}
        )

    fetches[0].wait()
    for t in range(tiles):
        x = v_ref[:, t * TILE:(t + 1) * TILE]
        top = jnp.max(x, axis=0, keepdims=True).astype(jnp.bfloat16).astype(jnp.float32)
        raw[h, t] = jnp.exp(x - top).astype(jnp.bfloat16)
        raw_top[h, t:t + 1, :] = top

    pl.semaphore_wait(barrier, len(peers) + n_st - 1)

    st_copies = []
    for d in range(1, n_st):
        other = lax.rem(h + d, n_st)
        for i, buf in enumerate((raw_top, raw)):
            st_copies.append(remote(
                buf.at[h], buf.at[h], st_send.at[d - 1, i], st_recv.at[d - 1, i], st=other))
            st_copies[-1].start()

    for fetch in fetches[1:]:
        fetch.wait()
    for a in range(n_dst):
        k = jnp.exp(-cost_ref[a]).astype(jnp.bfloat16)
        for b in range(n_org):
            kern_out[a, b] = k[:, b * rows:(b + 1) * rows]

    def cost_copy(a, dq):
        target = min(max(a, 1), last - 1)
        return remote(
            kern_out.at[a, lax.rem(q + dq, n_org)],
            kern_in.at[p, int(a != target), (n_org - dq) % n_org],
            k_send.at[a, dq], k_recv.at[int(a != target), p, (n_org - dq) % n_org],
            dst=target, org=lax.rem(q + dq, n_org))

    for a in range(n_dst):
        target = min(max(a, 1), last - 1)
        for dq in range(1, n_org):
            cost_copy(a, dq).start()

        @pl.when(p != target)
        def _(a=a):
            cost_copy(a, 0).start()

        @pl.when(p == target)
        def _(a=a, target=target):
            kern_in[p, int(a != target), 0] = kern_out[a, q]

    def cost_arrivals():
        for slot in range(2):
            for b in range(n_dst):
                for r in range(n_org):
                    @pl.when(active[slot] if r else active[slot] & (p != b))
                    def _(slot=slot, b=b, r=r):
                        place = kern_in.at[b, slot, r]
                        remote(place, place, k_send.at[0, 0], k_recv.at[slot, b, r],
                               dst=lax.rem(p + 1, n_dst)).wait_recv()

    for slot, r in ((i, j) for i in range(2) for j in range(n_org)):
        anchor = (served if slot else p) * n_org + lax.rem(q + r, n_org)
        count = counts_ref[anchor]
        for b in range(n_dst):
            block = b * n_org + q

            def listed(k, found, anchor=anchor, block=block, count=count):
                hit = jnp.where(lists_ref[k, anchor] == block, 1, 0)
                return found + hit * jnp.where(k < count, 1, 0)

            if slots <= 4:
                found = jnp.int32(0)
                for k in range(slots):
                    found = listed(k, found)
            else:
                found = lax.fori_loop(0, slots, listed, jnp.int32(0))
            reach[slot, r, b] = found.astype(jnp.float32)

    mine = trans_ref[:, pl.ds(pl.multiple_of(h * states, TILE), states)]
    low = jnp.bitwise_and(mine, TILE - 1)
    high = jnp.right_shift(mine, TILE.bit_length() - 1)
    for c in range(chunks):
        part = slice(c * width, (c + 1) * width)
        row_ids = lax.broadcasted_iota(jnp.int32, (TILE, width), 0)
        onehot[c] = jnp.where(row_ids == low[:, part], 1.0, 0.0).astype(jnp.bfloat16)

    for copy in st_copies:
        copy.wait_recv()

    total_tiles = n_st * tiles
    for c in range(chunks):
        part = slice(c * width, (c + 1) * width)
        table = raw_top[...].reshape(total_tiles, TILE).astype(jnp.bfloat16)
        picked = jnp.dot(table, onehot[c], preferred_element_type=jnp.float32)
        tile_ids = lax.broadcasted_iota(jnp.int32, (total_tiles, width), 0)
        tops[p, c] = jnp.sum(
            jnp.where(tile_ids == high[:, part], picked, 0.0), axis=0, keepdims=True)
    t_copies = []
    for d in range(1, n_dst):
        t_copies.append(remote(
            tops.at[p], tops.at[p], t_send.at[d - 1], t_recv.at[d - 1],
            dst=lax.rem(p + d, n_dst)))
        t_copies[-1].start()

    def gather(c):
        part = slice(c * width, (c + 1) * width)
        table = raw[...].reshape(total_tiles * rows, TILE)
        picked = jnp.dot(table, onehot[c], preferred_element_type=jnp.float32)
        total = picked[:rows]
        for t in range(1, total_tiles):
            total = jnp.where(high[:, part] == t, picked[t * rows:(t + 1) * rows], total)
        wbuf[p, c] = total.astype(jnp.bfloat16)

    def upward(b, c):
        return remote(wbuf.at[b, c], wbuf.at[b, c], up_send.at[b, c], w_recv.at[b, c],
                      dst=lax.rem(p + 1, n_dst))

    def downward(b, c):
        return remote(wbuf.at[b, c], wbuf.at[b, c], dn_send.at[b, c], w_recv.at[b, c],
                      dst=lax.rem(p + n_dst - 1, n_dst))

    can_up, can_down = p < last - 1, p > 1

    def send_own(c):
        @pl.when(can_up)
        def _():
            upward(p, c).start()

        @pl.when(can_down)
        def _():
            downward(p, c).start()

    def relay(d, c):
        @pl.when((p >= d) & inner)
        def _():
            upward(p - d, c).wait_recv()

        @pl.when((p >= d) & can_up)
        def _():
            upward(p - d, c).start()

        @pl.when((p + d < n_dst) & inner)
        def _():
            downward(p + d, c).wait_recv()

        @pl.when((p + d < n_dst) & can_down)
        def _():
            downward(p + d, c).start()

    def across(slot, r, c):
        at = (slot, r - 1, c)
        return [
            remote(source.at[at], target.at[at], x_send.at[slot, r - 1, c, i],
                   x_recv.at[slot, r - 1, c, i], org=lax.rem(q + r, n_org))
            for i, (source, target) in enumerate(((x_out_top, x_in_top), (x_out, x_in)))
        ]

    def outward(c):
        return [
            remote(source.at[c], target.at[c], z_send.at[c, i], z_recv.at[c, i], dst=served)
            for i, (source, target) in enumerate(((z_out_top, z_in_top), (z_out, z_in)))
        ]

    anchors = [(slot, r) for slot in range(2) for r in range(n_org)]

    def products(c):
        ceilings, scales = {}, {}
        for slot, r in anchors:
            shifted = [tops[b, c] + (reach[slot, r, b] - 1.0) * -FLOOR for b in range(n_dst)]
            ceiling = functools.reduce(jnp.maximum, shifted)
            ceilings[slot, r] = ceiling
            for b in range(n_dst):
                scales[slot, r, b] = reach[slot, r, b] * jnp.exp(shifted[b] - ceiling)
        totals = {}
        for b in range(n_dst):
            stacked = kern_in[b].reshape(len(anchors) * rows, rows)
            product = jnp.dot(stacked, wbuf[b, c], preferred_element_type=jnp.float32)
            for i, (slot, r) in enumerate(anchors):
                term = scales[slot, r, b] * product[i * rows:(i + 1) * rows]
                totals[slot, r] = totals[slot, r] + term if b else term
        for slot, r in anchors:
            if r == 0:
                own_sum[slot, c] = totals[slot, r]
                own_top[slot, c] = ceilings[slot, r]
            else:
                x_out[slot, r - 1, c] = totals[slot, r].astype(jnp.bfloat16)
                x_out_top[slot, r - 1, c] = ceilings[slot, r]
        for slot in (1, 0):
            @pl.when(active[slot])
            def _(slot=slot):
                for r in range(1, n_org):
                    for copy in across(slot, r, c):
                        copy.start()

    def finish(slot, c):
        for r in range(1, n_org):
            for copy in across(slot, r, c):
                copy.wait_recv()
        ceiling = own_top[slot, c]
        for r in range(1, n_org):
            ceiling = jnp.maximum(ceiling, x_in_top[slot, r - 1, c])
        merged = jnp.exp(own_top[slot, c] - ceiling) * own_sum[slot, c]
        for r in range(1, n_org):
            merged += (jnp.exp(x_in_top[slot, r - 1, c] - ceiling)
                       * x_in[slot, r - 1, c].astype(jnp.float32))
        if slot:
            z_out[c] = merged.astype(jnp.bfloat16)
            z_out_top[c] = ceiling
            for copy in outward(c):
                copy.start()
        else:
            out_ref[:, c * width:(c + 1) * width] = DISCOUNT * (ceiling + jnp.log(merged))

    def both(step, c):
        for slot in (1, 0):
            @pl.when(active[slot])
            def _(slot=slot):
                step(slot, c)

    for c in range(min(AHEAD, chunks)):
        gather(c)
        send_own(c)
    for c in range(AHEAD, chunks):
        gather(c)
    cost_arrivals()
    for copy in t_copies:
        copy.wait_recv()
    for wave in range(chunks + n_dst - 3):
        for d in range(1, n_dst - 1):
            c = wave - d + 1
            if 0 <= c < chunks:
                relay(d, c)
                if d == 1 and c + AHEAD < chunks:
                    send_own(c + AHEAD)
        done = wave - n_dst + 3
        if done >= 0:
            @pl.when(inner)
            def _(done=done):
                products(done)
        if done >= 1:
            both(finish, done - 1)
    both(finish, chunks - 1)

    @pl.when(jnp.logical_not(inner))
    def _():
        for c in range(chunks):
            for copy in outward(c):
                copy.wait_recv()
            out_ref[:, c * width:(c + 1) * width] = DISCOUNT * (
                z_in_top[c] + jnp.log(z_in[c].astype(jnp.float32)))

    for copy in st_copies + t_copies:
        copy.wait_send()
    for a in range(n_dst):
        for dq in range(1, n_org):
            cost_copy(a, dq).wait_send()

        @pl.when(p != min(max(a, 1), last - 1))
        def _(a=a):
            cost_copy(a, 0).wait_send()

    for c in range(chunks):
        for d in range(n_dst):
            @pl.when((p >= d) & can_up)
            def _(d=d, c=c):
                upward(p - d, c).wait_send()

            @pl.when((p + d < n_dst) & can_down)
            def _(d=d, c=c):
                downward(p + d, c).wait_send()

        for slot in range(2):
            @pl.when(active[slot])
            def _(slot=slot, c=c):
                copies = [copy for r in range(1, n_org) for copy in across(slot, r, c)]
                for copy in copies + (outward(c) if slot else []):
                    copy.wait_send()


def on_device(sizes, value_now, utility, move_costs, dest_blocks, row_counts, transition):
    n_dst, n_org, n_st = sizes
    rows, states = value_now.shape[2:]
    width = min(CHUNK, states)
    chunks = states // width
    tiles = states // TILE
    others = max(n_org - 1, 1)
    vmem = pl.BlockSpec(memory_space=pltpu.VMEM)
    hbm = pl.BlockSpec(memory_space=pltpu.HBM)
    dma = pltpu.SemaphoreType.DMA
    bf16, f32 = jnp.bfloat16, jnp.float32
    partial = pl.pallas_call(
        functools.partial(sweep, sizes),
        out_shape=jax.ShapeDtypeStruct((rows, states), f32),
        in_specs=[hbm] * 5,
        out_specs=vmem,
        scratch_shapes=[
            pltpu.VMEM((rows, states), f32),
            pltpu.VMEM((n_dst, rows, n_org * rows), f32),
            pltpu.VMEM((1, transition.shape[0]), jnp.int32),
            pltpu.SMEM(dest_blocks.shape[::-1], jnp.int32),
            pltpu.SMEM(row_counts.shape, jnp.int32),
            dma((5,)),
            pltpu.VMEM((n_st, tiles, rows, TILE), bf16),
            pltpu.VMEM((n_st, tiles, TILE), f32),
            pltpu.VMEM((n_dst, n_org, rows, rows), bf16),
            pltpu.VMEM((n_dst, 2, n_org, rows, rows), bf16),
            pltpu.VMEM((chunks, TILE, width), bf16),
            pltpu.VMEM((n_dst, chunks, rows, width), bf16),
            pltpu.VMEM((n_dst, chunks, 1, width), f32),
            pltpu.VMEM((2, chunks, rows, width), f32),
            pltpu.VMEM((2, chunks, 1, width), f32),
            pltpu.VMEM((2, others, chunks, rows, width), bf16),
            pltpu.VMEM((2, others, chunks, 1, width), f32),
            pltpu.VMEM((2, others, chunks, rows, width), bf16),
            pltpu.VMEM((2, others, chunks, 1, width), f32),
            pltpu.VMEM((chunks, rows, width), bf16),
            pltpu.VMEM((chunks, 1, width), f32),
            pltpu.VMEM((chunks, rows, width), bf16),
            pltpu.VMEM((chunks, 1, width), f32),
            pltpu.SMEM((2, n_org, n_dst), f32),
            dma((max(n_st - 1, 1), 2)), dma((max(n_st - 1, 1), 2)),
            dma((n_dst, n_org)), dma((2, n_dst, n_org)),
            dma((max(n_dst - 1, 1),)), dma((max(n_dst - 1, 1),)),
            dma((n_dst, chunks)), dma((n_dst, chunks)), dma((n_dst, chunks)),
            dma((2, others, chunks, 2)), dma((2, others, chunks, 2)),
            dma((chunks, 2)), dma((chunks, 2)),
        ],
        compiler_params=pltpu.CompilerParams(
            collective_id=0, has_side_effects=True, vmem_limit_bytes=63 * 2**20
        ),
    )(
        value_now.reshape(rows, states),
        move_costs.reshape(n_dst, rows, n_org * rows),
        transition.reshape(1, -1),
        dest_blocks.T,
        row_counts,
    )
    return utility + partial[None, None]


def solution(mesh):
    sizes = tuple(mesh.shape[axis] for axis in ("dst", "org", "st"))
    return jax.shard_map(
        functools.partial(on_device, sizes),
        mesh=mesh,
        in_specs=(
            P(("draws", "dst"), "org", None, "st"),
            P(("draws", "dst"), "org", None, "st"),
            P("draws", "org", None, "dst", None),
            P(),
            P(),
            P(),
        ),
        out_specs=P(("draws", "dst"), "org", None, "st"),
        check_vma=False,
    )
```

```python
import functools

import jax
import jax.numpy as jnp
from jax import lax
from jax.experimental import pallas as pl
from jax.experimental.pallas import tpu as pltpu
from jax.sharding import PartitionSpec as P

DISCOUNT = 0.95
FLOOR = -1e30
TILE = 256
CHUNK = 512
AHEAD = 2
MESH = pl.DeviceIdType.MESH


def sweep(
    sizes, v_in, cost_in, trans_in, lists_in, counts_in, out_ref,
    v_ref, cost_ref, trans_ref, lists_ref, counts_ref, in_sem,
    raw, raw_top, kern_out, kern_in, onehot, wbuf, tops, own_sum, own_top,
    x_out, x_out_top, x_in, x_in_top, reach,
    st_send, st_recv, k_send, k_recv, t_send, t_recv, up_send, dn_send, w_recv, x_send, x_recv,
):
    n_dst, n_org, n_st = sizes
    rows, states = v_ref.shape
    tiles = states // TILE
    chunks, width = wbuf.shape[1], wbuf.shape[3]
    slots = lists_ref.shape[0]
    p = lax.axis_index("dst")
    q = lax.axis_index("org")
    h = lax.axis_index("st")

    def remote(source, target, send, recv, **where):
        return pltpu.make_async_remote_copy(
            src_ref=source, dst_ref=target, send_sem=send, recv_sem=recv,
            device_id=where, device_id_type=MESH,
        )

    fetches = [
        pltpu.make_async_copy(source, target, in_sem.at[i])
        for i, (source, target) in enumerate((
            (v_in, v_ref), (cost_in, cost_ref), (trans_in, trans_ref),
            (lists_in, lists_ref), (counts_in, counts_ref)))
    ]
    for fetch in fetches:
        fetch.start()
    peers = [(a, b) for a in range(n_dst) for b in range(n_org) if (a, b) != (0, 0)]
    barrier = pltpu.get_barrier_semaphore()
    for dp, dq in peers:
        pl.semaphore_signal(
            barrier, inc=1, device_id_type=MESH,
            device_id={"dst": lax.rem(p + dp, n_dst), "org": lax.rem(q + dq, n_org)},
        )
    for d in range(1, n_st):
        pl.semaphore_signal(
            barrier, inc=1, device_id_type=MESH, device_id={"st": lax.rem(h + d, n_st)}
        )

    fetches[0].wait()
    for t in range(tiles):
        x = v_ref[:, t * TILE:(t + 1) * TILE]
        top = jnp.max(x, axis=0, keepdims=True).astype(jnp.bfloat16).astype(jnp.float32)
        raw[h, t] = jnp.exp(x - top).astype(jnp.bfloat16)
        raw_top[h, t:t + 1, :] = top

    pl.semaphore_wait(barrier, len(peers) + n_st - 1)

    st_copies = []
    for d in range(1, n_st):
        other = lax.rem(h + d, n_st)
        for i, buf in enumerate((raw_top, raw)):
            st_copies.append(remote(
                buf.at[h], buf.at[h], st_send.at[d - 1, i], st_recv.at[d - 1, i], st=other))
            st_copies[-1].start()

    for fetch in fetches[1:]:
        fetch.wait()
    for a in range(n_dst):
        k = jnp.exp(-cost_ref[a]).astype(jnp.bfloat16)
        for b in range(n_org):
            kern_out[a, b] = k[:, b * rows:(b + 1) * rows]
    k_copies = []
    for i, (dp, dq) in enumerate(peers):
        to_p, to_q = lax.rem(p + dp, n_dst), lax.rem(q + dq, n_org)
        k_copies.append(remote(
            kern_out.at[to_p, to_q], kern_in.at[p, (n_org - dq) % n_org],
            k_send.at[i], k_recv.at[i], dst=to_p, org=to_q))
        k_copies[-1].start()
    kern_in[p, 0] = kern_out[p, q]

    for r in range(n_org):
        anchor = p * n_org + lax.rem(q + r, n_org)
        count = counts_ref[anchor]
        for b in range(n_dst):
            block = b * n_org + q

            def listed(k, found, anchor=anchor, block=block, count=count):
                hit = jnp.where(lists_ref[k, anchor] == block, 1, 0)
                return found + hit * jnp.where(k < count, 1, 0)

            if slots <= 4:
                found = jnp.int32(0)
                for k in range(slots):
                    found = listed(k, found)
            else:
                found = lax.fori_loop(0, slots, listed, jnp.int32(0))
            reach[r, b] = found.astype(jnp.float32)

    mine = trans_ref[:, pl.ds(pl.multiple_of(h * states, TILE), states)]
    low = jnp.bitwise_and(mine, TILE - 1)
    high = jnp.right_shift(mine, TILE.bit_length() - 1)
    for c in range(chunks):
        part = slice(c * width, (c + 1) * width)
        row_ids = lax.broadcasted_iota(jnp.int32, (TILE, width), 0)
        onehot[c] = jnp.where(row_ids == low[:, part], 1.0, 0.0).astype(jnp.bfloat16)

    for copy in st_copies:
        copy.wait_recv()

    total_tiles = n_st * tiles
    for c in range(chunks):
        part = slice(c * width, (c + 1) * width)
        table = raw_top[...].reshape(total_tiles, TILE).astype(jnp.bfloat16)
        picked = jnp.dot(table, onehot[c], preferred_element_type=jnp.float32)
        tile_ids = lax.broadcasted_iota(jnp.int32, (total_tiles, width), 0)
        tops[p, c] = jnp.sum(
            jnp.where(tile_ids == high[:, part], picked, 0.0), axis=0, keepdims=True)
    t_copies = []
    for d in range(1, n_dst):
        t_copies.append(remote(
            tops.at[p], tops.at[p], t_send.at[d - 1], t_recv.at[d - 1],
            dst=lax.rem(p + d, n_dst)))
        t_copies[-1].start()

    def gather(c):
        part = slice(c * width, (c + 1) * width)
        table = raw[...].reshape(total_tiles * rows, TILE)
        picked = jnp.dot(table, onehot[c], preferred_element_type=jnp.float32)
        total = picked[:rows]
        for t in range(1, total_tiles):
            total = jnp.where(high[:, part] == t, picked[t * rows:(t + 1) * rows], total)
        wbuf[p, c] = total.astype(jnp.bfloat16)

    def upward(b, c):
        return remote(wbuf.at[b, c], wbuf.at[b, c], up_send.at[b, c], w_recv.at[b, c],
                      dst=lax.rem(p + 1, n_dst))

    def downward(b, c):
        return remote(wbuf.at[b, c], wbuf.at[b, c], dn_send.at[b, c], w_recv.at[b, c],
                      dst=lax.rem(p + n_dst - 1, n_dst))

    not_last, not_first = p < n_dst - 1, p > 0

    def send_own(c):
        @pl.when(not_last)
        def _():
            upward(p, c).start()

        @pl.when(not_first)
        def _():
            downward(p, c).start()

    def relay(d, c):
        @pl.when(p >= d)
        def _():
            upward(p - d, c).wait_recv()

        @pl.when((p >= d) & not_last)
        def _():
            upward(p - d, c).start()

        @pl.when(p + d < n_dst)
        def _():
            downward(p + d, c).wait_recv()

        @pl.when((p + d < n_dst) & not_first)
        def _():
            downward(p + d, c).start()

    x_copies = {}

    def products(c):
        ceilings, scales, totals = [], [], []
        for r in range(n_org):
            shifted = [tops[b, c] + (reach[r, b] - 1.0) * -FLOOR for b in range(n_dst)]
            ceilings.append(functools.reduce(jnp.maximum, shifted))
            scales.append([reach[r, b] * jnp.exp(shifted[b] - ceilings[r]) for b in range(n_dst)])
        for b in range(n_dst):
            stacked = kern_in[b].reshape(n_org * rows, rows)
            product = jnp.dot(stacked, wbuf[b, c], preferred_element_type=jnp.float32)
            terms = [scales[r][b] * product[r * rows:(r + 1) * rows] for r in range(n_org)]
            totals = [x + y for x, y in zip(totals, terms)] if b else terms
        own_sum[c] = totals[0]
        own_top[c] = ceilings[0]
        for r in range(1, n_org):
            x_out[r - 1, c] = totals[r].astype(jnp.bfloat16)
            x_out_top[r - 1, c] = ceilings[r]
            to = lax.rem(q + r, n_org)
            for i, (src, dst) in enumerate(((x_out_top, x_in_top), (x_out, x_in))):
                copy = remote(src.at[r - 1, c], dst.at[r - 1, c],
                              x_send.at[r - 1, c, i], x_recv.at[r - 1, c, i], org=to)
                copy.start()
                x_copies.setdefault(c, []).append(copy)

    def finish(c):
        for copy in x_copies.get(c, []):
            copy.wait_recv()
        ceiling = own_top[c]
        for r in range(1, n_org):
            ceiling = jnp.maximum(ceiling, x_in_top[r - 1, c])
        merged = jnp.exp(own_top[c] - ceiling) * own_sum[c]
        for r in range(1, n_org):
            merged += jnp.exp(x_in_top[r - 1, c] - ceiling) * x_in[r - 1, c].astype(jnp.float32)
        out_ref[:, c * width:(c + 1) * width] = DISCOUNT * (ceiling + jnp.log(merged))

    for c in range(min(AHEAD, chunks)):
        gather(c)
        send_own(c)
    for c in range(AHEAD, chunks):
        gather(c)
    for copy in k_copies:
        copy.wait_recv()
    for copy in t_copies:
        copy.wait_recv()
    for wave in range(chunks + n_dst - 2):
        for d in range(1, n_dst):
            c = wave - d + 1
            if 0 <= c < chunks:
                relay(d, c)
                if d == 1 and c + AHEAD < chunks:
                    send_own(c + AHEAD)
        done = wave - n_dst + 2
        if done >= 0:
            products(done)
        if done >= 1:
            finish(done - 1)
    finish(chunks - 1)

    for copy in st_copies + k_copies + t_copies:
        copy.wait_send()
    for c in range(chunks):
        for d in range(n_dst):
            @pl.when((p >= d) & not_last)
            def _(d=d, c=c):
                upward(p - d, c).wait_send()

            @pl.when((p + d < n_dst) & not_first)
            def _(d=d, c=c):
                downward(p + d, c).wait_send()

        for copy in x_copies.get(c, []):
            copy.wait_send()


def on_device(sizes, value_now, utility, move_costs, dest_blocks, row_counts, transition):
    n_dst, n_org, n_st = sizes
    rows, states = value_now.shape[2:]
    width = min(CHUNK, states)
    chunks = states // width
    tiles = states // TILE
    peers = n_dst * n_org - 1
    others = max(n_org - 1, 1)
    vmem = pl.BlockSpec(memory_space=pltpu.VMEM)
    hbm = pl.BlockSpec(memory_space=pltpu.HBM)
    dma = pltpu.SemaphoreType.DMA
    bf16, f32 = jnp.bfloat16, jnp.float32
    partial = pl.pallas_call(
        functools.partial(sweep, sizes),
        out_shape=jax.ShapeDtypeStruct((rows, states), f32),
        in_specs=[hbm] * 5,
        out_specs=vmem,
        scratch_shapes=[
            pltpu.VMEM((rows, states), f32),
            pltpu.VMEM((n_dst, rows, n_org * rows), f32),
            pltpu.VMEM((1, transition.shape[0]), jnp.int32),
            pltpu.SMEM(dest_blocks.shape[::-1], jnp.int32),
            pltpu.SMEM(row_counts.shape, jnp.int32),
            dma((5,)),
            pltpu.VMEM((n_st, tiles, rows, TILE), bf16),
            pltpu.VMEM((n_st, tiles, TILE), f32),
            pltpu.VMEM((n_dst, n_org, rows, rows), bf16),
            pltpu.VMEM((n_dst, n_org, rows, rows), bf16),
            pltpu.VMEM((chunks, TILE, width), bf16),
            pltpu.VMEM((n_dst, chunks, rows, width), bf16),
            pltpu.VMEM((n_dst, chunks, 1, width), f32),
            pltpu.VMEM((chunks, rows, width), f32),
            pltpu.VMEM((chunks, 1, width), f32),
            pltpu.VMEM((others, chunks, rows, width), bf16),
            pltpu.VMEM((others, chunks, 1, width), f32),
            pltpu.VMEM((others, chunks, rows, width), bf16),
            pltpu.VMEM((others, chunks, 1, width), f32),
            pltpu.SMEM((n_org, n_dst), f32),
            dma((max(n_st - 1, 1), 2)), dma((max(n_st - 1, 1), 2)),
            dma((max(peers, 1),)), dma((max(peers, 1),)),
            dma((max(n_dst - 1, 1),)), dma((max(n_dst - 1, 1),)),
            dma((n_dst, chunks)), dma((n_dst, chunks)), dma((n_dst, chunks)),
            dma((others, chunks, 2)), dma((others, chunks, 2)),
        ],
        compiler_params=pltpu.CompilerParams(
            collective_id=0, has_side_effects=True, vmem_limit_bytes=63 * 2**20
        ),
    )(
        value_now.reshape(rows, states),
        move_costs.reshape(n_dst, rows, n_org * rows),
        transition.reshape(1, -1),
        dest_blocks.T,
        row_counts,
    )
    return utility + partial[None, None]


def solution(mesh):
    sizes = tuple(mesh.shape[axis] for axis in ("dst", "org", "st"))
    return jax.shard_map(
        functools.partial(on_device, sizes),
        mesh=mesh,
        in_specs=(
            P(("draws", "dst"), "org", None, "st"),
            P(("draws", "dst"), "org", None, "st"),
            P("draws", "org", None, "dst", None),
            P(),
            P(),
            P(),
        ),
        out_specs=P(("draws", "dst"), "org", None, "st"),
        check_vma=False,
    )
```
